32 devices in a mesh: tm: 16 (over z, y, core), region: 2 (over x).
Axes of the slice: x: 2, y: 2, z: 4, core: 2. Of those that a mesh axis runs over, the one named last changes fastest.
Arguments:
- waveform: bfloat16 [192, 131072], P('region', 'tm'), may hold values from -220 to 220
- station_order: int32 [192], P('region'), may hold values from 0 to 191, each once
- library: float32 [128, 24, 200], P('tm'), may hold values from -6 to 6
- owner: int32 [4], replicated, may hold values from 0 to 15
- channels: int32 [4, 8, 24], replicated, may hold values from 0 to 191, as said below
Outputs:
- detection: float32 [4, 8, 131072], P(None, 'region', 'tm')
The draws below stay inside these ranges and needn't reach their ends.
Inputs may be any that keep to these rules, and one draw needn't show every extreme that they name: `channels`: within one template the 24 station channel ids differ.
All inputs are finite; a program needn't handle non-finite values.
Results may differ from the reference program's by a relative error of at most 0.003.
Values may be sent and summed in bfloat16 or wider, within the bound.
A program may use at most 64 MiB of HBM per device.

```python
import math
import jax
import jax.numpy as jnp
from jax import lax

CH = 192
TCH = 24
TAPS = 200
NTPL = 8
STEPS = 4
TIME = 131072
LIB = 128
N_TM = 16
N_REGION = 2


def draw_waveform(key, part):
    key_noise = jax.random.fold_in(key, 11)
    key_gain = jax.random.fold_in(key, 12)
    key_phase = jax.random.fold_in(key, 13)
    times = jnp.arange(TIME, dtype=jnp.int32)
    fraction = times.astype(jnp.float32)[None, :] / TIME
    channel_gain = jnp.exp(jax.random.uniform(key_gain, (CH, 1), jnp.float32, math.log(0.5), math.log(3.4)))
    starts = jax.random.randint(key_phase, (2,), 0, 4096, jnp.int32)
    period_one = TAPS // 5 + 1
    period_two = TAPS // 9 + 2
    angle_one = ((times + starts[0]) % period_one).astype(jnp.float32) * (2.0 * math.pi / period_one)
    angle_two = ((times + starts[1]) % period_two).astype(jnp.float32) * (2.0 * math.pi / period_two)
    shared = (jnp.sin(angle_one) + jnp.sin(angle_two))[None, :]
    random_part = jax.random.truncated_normal(key_noise, -3.0, 3.0, (CH, TIME), jnp.float32)
    envelope = jnp.exp(math.log(12.0) * fraction)
    values = channel_gain * envelope * (random_part + 0.8 * shared)
    return values.astype(jnp.bfloat16)


def draw_channels(key, part):
    row_keys = jax.random.split(jax.random.fold_in(key, 21), STEPS * NTPL)
    chosen = jax.vmap(lambda row_key: jax.random.permutation(row_key, CH)[:TCH])(row_keys).astype(jnp.int32)
    remainder = jax.random.permutation(jax.random.fold_in(key, 22), CH - 2)[:TCH - 2].astype(jnp.int32) + 1
    leading = jnp.concatenate([jnp.array([0, CH - 1], jnp.int32), remainder])
    chosen = chosen.at[0].set(leading)
    return chosen.reshape(STEPS, NTPL, TCH).astype(jnp.int32)


def touch_ends(entries, key, low, high):
    place = [jax.random.randint(jax.random.fold_in(key, axis), (), 0, length) for axis, length in enumerate(entries.shape)]
    longest = entries.shape.index(max(entries.shape))
    neighbour = place[:longest] + [(place[longest] + 1) % entries.shape[longest]] + place[longest + 1:]
    return entries.at[tuple(place)].set(low).at[tuple(neighbour)].set(high)


def block_scale(own_key, dims, shards, least, largest):
    loudness, own = 1.0, jax.random.fold_in(own_key, 6)
    for axis_at, blocks in shards:
        heights = jnp.exp(jax.random.uniform(jax.random.fold_in(own, axis_at), (blocks,), jnp.float32, least / len(shards), largest / len(shards)))
        loudness = loudness * jnp.repeat(heights, dims[axis_at] // blocks).reshape([-1 if axis == axis_at else 1 for axis in range(len(dims))])
    return loudness


def gaussian(rng, dims, scale, bound, shards=(), held_as=jnp.bfloat16):
    values = scale * jax.random.normal(rng, dims, jnp.float32)
    if shards:
        values = values * block_scale(rng, dims, shards, -0.22, 0.18)
    return jnp.clip(values, -bound, bound).astype(held_as)


def setup_inputs(seed: int = 0) -> dict:
    arg_keys = jax.random.split(jax.random.key(seed), 6)
    return {
        "waveform": draw_waveform(jax.random.fold_in(arg_keys[5], 71), 0),
        "station_order": jax.random.permutation(arg_keys[1], CH).astype(jnp.int32),
        "library": gaussian(arg_keys[2], (LIB, TCH, TAPS), 1.0, 6.0, ((0, 16),), jnp.float32),
        "owner": touch_ends(jax.random.randint(arg_keys[3], (STEPS,), 0, N_TM), jax.random.fold_in(arg_keys[3], 1), 0, N_TM - 1).astype(jnp.int32),
        "channels": draw_channels(jax.random.fold_in(arg_keys[5], 71), 0),
    }


water_level = 4.0
eps = 1e-06

def reference(waveform, station_order, library, owner, channels):
    padded = jnp.pad(waveform, ((0, 0), (0, TAPS - 1)))
    squares = padded.astype(jnp.float32) ** 2

    def add_square(tap_index, running):
        return running + lax.dynamic_slice_in_dim(squares, tap_index, TIME, 1)
    energy = lax.fori_loop(0, TAPS, add_square, jnp.zeros((CH, TIME), jnp.float32))
    inv_scale = 1.0 / jnp.sqrt(energy + TAPS * water_level)
    where_col = jnp.zeros((CH,), jnp.int32).at[station_order].set(jnp.arange(CH, dtype=jnp.int32))
    per_region = CH // N_REGION
    region_of = (where_col // per_region).astype(jnp.int32)
    region_onehot = (region_of[:, None] == jnp.arange(N_REGION, dtype=jnp.int32)[None, :]).astype(jnp.float32)
    outputs = []
    for step_index in range(STEPS):
        first_row = (owner[step_index] * NTPL).astype(jnp.int32)
        panel = lax.dynamic_slice_in_dim(library, first_row, NTPL, 0)
        centred = panel - lax.optimization_barrier(jnp.mean(panel, axis=2, keepdims=True))
        norm_taps = (centred / jnp.sqrt(lax.optimization_barrier(jnp.sum(centred * centred, axis=2, keepdims=True)) + eps)).astype(jnp.bfloat16)
        taps_wide = norm_taps.astype(jnp.float32)
        stations = channels[step_index]
        columns = where_col[stations]
        rows_data = padded[columns].astype(jnp.float32)

        def add_product(tap_index, running):
            weight = lax.dynamic_slice_in_dim(taps_wide, tap_index, 1, 2)
            return running + weight * lax.dynamic_slice_in_dim(rows_data, tap_index, TIME, 2)
        summed = lax.fori_loop(0, TAPS, add_product, jnp.zeros((NTPL, TCH, TIME), jnp.float32))
        correlation = summed * inv_scale[columns]
        partial_value = jnp.einsum('kjt,kjr->krt', correlation, region_onehot[columns], precision=lax.Precision.HIGHEST)
        stacked = lax.optimization_barrier(jnp.sum(partial_value, axis=1))
        mean_power = lax.optimization_barrier(jnp.sum(stacked * stacked, axis=1, keepdims=True)) / TIME + eps
        outputs.append(stacked / jnp.sqrt(mean_power))
    return jnp.stack(outputs)
```

```python
import functools
import jax
import jax.numpy as jnp
from jax import lax
from jax.experimental import pallas as pl
from jax.experimental.pallas import tpu as pltpu
from jax.sharding import PartitionSpec as P

water_level = 4.0
eps = 1e-06
unroll = 4


def scale_kernel(taps, x_ref, inv_ref):
    chans = x_ref.shape[0]
    rows = x_ref.shape[1]
    step = 4
    offsets = lax.broadcasted_iota(jnp.int32, (384, 128), 0) - lax.broadcasted_iota(jnp.int32, (384, 128), 1)
    band = ((offsets >= 0) & (offsets < taps)).astype(jnp.float32).astype(jnp.bfloat16)

    def chunk(i, carry):
        x = x_ref[pl.ds(i * step, step)].reshape(step * rows, 384).astype(jnp.float32)
        square = x * x
        high = square.astype(jnp.bfloat16)
        low = (square - high.astype(jnp.float32)).astype(jnp.bfloat16)
        energy = jnp.dot(high, band, preferred_element_type=jnp.float32)
        energy = energy + jnp.dot(low, band, preferred_element_type=jnp.float32)
        inv_ref[pl.ds(i * step, step)] = lax.rsqrt(energy + taps * water_level).reshape(step, rows, 128)
        return carry

    lax.fori_loop(0, chans // step, chunk, 0)


def pair_kernel(count_ref, code_ref, x_ref, inv_ref, taps_ref, out_ref, acc_ref):
    templates = out_ref.shape[0]
    acc_ref[...] = jnp.zeros_like(acc_ref)
    lane = lax.broadcasted_iota(jnp.int32, (8, 128), 1)
    sub = lax.broadcasted_iota(jnp.int32, (8, 128), 0)

    def one_pair(code):
        template = code & 63
        col = (code >> 6) & 255
        row = code >> 14
        taps = taps_ref[pl.ds(row, 1), :]
        first = jnp.broadcast_to(taps[:, :128], (8, 128))
        second = jnp.broadcast_to(taps[:, 128:], (8, 128))
        first = pltpu.roll(first, 1, 1, stride=1, stride_axis=0)
        second = pltpu.roll(second, 1, 1, stride=1, stride_axis=0)
        zero = jnp.zeros((8, 128), jnp.float32)
        parts = [[], [], []]
        for a in range(16):
            one = pltpu.roll(first, 8 * a, 1) if a else first
            two = pltpu.roll(second, 8 * a, 1) if a else second
            below = lane <= sub + 8 * a
            parts[0].append(jnp.where(below, two, zero))
            parts[1].append(jnp.where(below, one, two))
            parts[2].append(jnp.where(below, zero, one))
        matrix = jnp.concatenate(parts[0] + parts[1] + parts[2], axis=0).astype(jnp.bfloat16)
        product = jnp.dot(x_ref[col], matrix, preferred_element_type=jnp.float32)
        return template, product * inv_ref[col]

    def group(i, carry):
        done = [one_pair(code_ref[i * unroll + u]) for u in range(unroll)]
        for template, value in done:
            acc_ref[template] += value
        return carry

    lax.fori_loop(0, (count_ref[0] + unroll - 1) // unroll, group, 0)
    out_ref[...] = acc_ref[:templates]


def summed_over(value, axis):
    count = lax.axis_size(axis)
    me = lax.axis_index(axis)
    bits = [1 << b for b in range(count.bit_length() - 1)]

    def swap(block, bit):
        return lax.ppermute(block, axis, [(i, i ^ bit) for i in range(count)])

    for bit in bits:
        half = value.shape[0] // 2
        low, high = value[:half], value[half:]
        upper = (me & bit) > 0
        value = jnp.where(upper, high, low) + swap(jnp.where(upper, low, high), bit)
    for bit in reversed(bits):
        upper = (me & bit) > 0
        other = swap(value, bit)
        value = jnp.concatenate([jnp.where(upper, other, value), jnp.where(upper, value, other)], axis=0)
    return value


def finish_kernel(total_time, count, parts_ref, out_ref, sent, got, send_sems, recv_sems):
    me = lax.axis_index("tm")
    region = lax.axis_index("region")
    barrier = pltpu.get_barrier_semaphore()
    for d in range(1, count):
        peer = lax.rem(me + d, count)
        pl.semaphore_signal(barrier, inc=1, device_id=(peer, region), device_id_type=pl.DeviceIdType.MESH)
    held = out_ref.shape[0]
    stacked = parts_ref[0]
    for p in range(1, parts_ref.shape[0]):
        stacked = stacked + parts_ref[p]
    out_ref[...] = stacked
    power = jnp.sum(stacked * stacked, axis=1)
    power = jnp.broadcast_to(jnp.sum(power, axis=1, keepdims=True), (held, 128))
    sent[...] = power
    pl.semaphore_wait(barrier, count - 1)
    copies = []
    for d in range(1, count):
        peer = lax.rem(me + d, count)
        copy = pltpu.make_async_remote_copy(
            src_ref=sent,
            dst_ref=got.at[d - 1],
            send_sem=send_sems.at[d - 1],
            recv_sem=recv_sems.at[d - 1],
            device_id=(peer, region),
            device_id_type=pl.DeviceIdType.MESH,
        )
        copy.start()
        copies.append(copy)
    for copy in copies:
        copy.wait()
    power = power + jnp.sum(got[...], axis=0)
    factor = lax.rsqrt(power / total_time + eps)
    out_ref[...] = out_ref[...] * factor[:, None, :]


def pair_lists(station_order, channels, groups):
    steps, templates, used = channels.shape
    per_group = templates // groups
    length = steps * per_group * used
    grouped = channels.reshape(steps, groups, per_group, used).transpose(1, 0, 2, 3).reshape(groups, length)
    slot = jnp.arange(length, dtype=jnp.int32)
    step = slot // (per_group * used)
    inner = slot % (per_group * used)
    match = (grouped[:, :, None] == station_order[None, None, :]).astype(jnp.int32)
    local = jnp.sum(match, axis=2)
    col = jnp.sum(match * jnp.arange(station_order.shape[0], dtype=jnp.int32), axis=2)
    before = (slot[:, None] > slot[None, :]).astype(jnp.int32)
    place = jnp.sum(before[None] * local[:, None, :], axis=2)
    count = jnp.sum(local, axis=1)
    row = step * (templates * used) + jnp.arange(groups, dtype=jnp.int32)[:, None] * (per_group * used) + inner
    template = slot // used
    code = (row << 14) | (col << 6) | template
    chosen = ((place[:, None, :] == slot[None, :, None]) & (local[:, None, :] > 0)).astype(jnp.int32)
    packed = jnp.sum(chosen * code[:, None, :], axis=2)
    packed = jnp.where(slot[None, :] < count[:, None], packed, steps * per_group)
    return packed, count


def body(waveform, station_order, library, owner, channels):
    chan_local, time_local = waveform.shape
    num_blocks = time_local // 128
    steps, templates, used = channels.shape
    tap_count = library.shape[2]
    tm_size = lax.axis_size("tm")
    regions = lax.axis_size("region")
    per_group = templates // regions
    held = steps * per_group
    total_time = time_local * tm_size

    rim = lax.ppermute(waveform[:, :256], "tm", [(i, i - 1) for i in range(1, tm_size)])
    rim = jnp.where(jnp.arange(256)[None, :] < tap_count - 1, rim, jnp.zeros_like(rim))

    centred = library - jnp.mean(library, axis=2, keepdims=True)
    normed = centred / jnp.sqrt(jnp.sum(centred * centred, axis=2, keepdims=True) + eps)
    normed = jnp.pad(normed.astype(jnp.bfloat16).reshape(templates * used, tap_count), ((0, 0), (0, 256 - tap_count)))
    mine = (owner == lax.axis_index("tm"))[:, None, None]
    taps = jnp.where(mine, normed[None], jnp.zeros_like(normed)[None])
    taps = summed_over(taps.reshape(steps * templates * used, 256), "tm")
    taps = jnp.flip(taps, axis=1).astype(jnp.float32)

    blocked = waveform.reshape(chan_local, num_blocks, 128)
    rim_blocks = rim.reshape(chan_local, 2, 128)
    extended = jnp.concatenate([blocked, rim_blocks], axis=1)
    windows = jnp.concatenate([extended[:, i : i + num_blocks] for i in range(3)], axis=2)

    vmem = pl.BlockSpec(memory_space=pltpu.VMEM)
    smem = pl.BlockSpec(memory_space=pltpu.SMEM)
    inv_scale = pl.pallas_call(
        functools.partial(scale_kernel, tap_count),
        out_shape=jax.ShapeDtypeStruct((chan_local, num_blocks, 128), jnp.float32),
        in_specs=[vmem],
        out_specs=vmem,
        compiler_params=pltpu.CompilerParams(vmem_limit_bytes=40 * 2**20),
        name="scales",
    )(windows)

    codes, counts = pair_lists(station_order, channels, regions)
    me = lax.axis_index("region")

    def partial_sums(group):
        return pl.pallas_call(
            pair_kernel,
            out_shape=jax.ShapeDtypeStruct((held, num_blocks, 128), jnp.float32),
            in_specs=[smem, smem, vmem, vmem, vmem],
            out_specs=vmem,
            scratch_shapes=[pltpu.VMEM((held + 1, num_blocks, 128), jnp.float32)],
            compiler_params=pltpu.CompilerParams(vmem_limit_bytes=40 * 2**20),
            cost_estimate=pl.CostEstimate(flops=held * used * 64 * 384 * 256, bytes_accessed=9 * 2**20, transcendentals=0),
            name="pairs",
        )(lax.dynamic_slice_in_dim(counts, group, 1), lax.dynamic_index_in_dim(codes, group, 0, False), windows, inv_scale, taps)

    arrived = []
    for shift in range(1, regions):
        part = partial_sums((me + shift) % regions)
        arrived.append(lax.ppermute(part, "region", [(i, (i + shift) % regions) for i in range(regions)]))
    arrived.append(partial_sums(me))
    result = pl.pallas_call(
        functools.partial(finish_kernel, total_time, tm_size),
        out_shape=jax.ShapeDtypeStruct((held, num_blocks, 128), jnp.float32),
        in_specs=[vmem],
        out_specs=vmem,
        scratch_shapes=[
            pltpu.VMEM((held, 128), jnp.float32),
            pltpu.VMEM((tm_size - 1, held, 128), jnp.float32),
            pltpu.SemaphoreType.DMA((tm_size - 1,)),
            pltpu.SemaphoreType.DMA((tm_size - 1,)),
        ],
        compiler_params=pltpu.CompilerParams(
            collective_id=0, has_side_effects=True, vmem_limit_bytes=40 * 2**20
        ),
        name="finish",
    )(jnp.stack(arrived))
    return result.reshape(steps, per_group, time_local)


def solution(mesh):
    in_specs = (P("region", "tm"), P("region"), P("tm", None, None), P(), P())
    out_specs = P(None, "region", "tm")
    return jax.shard_map(body, mesh=mesh, in_specs=in_specs, out_specs=out_specs, check_vma=False)
```

```python
import functools
import jax
import jax.numpy as jnp
from jax import lax
from jax.experimental import pallas as pl
from jax.experimental.pallas import tpu as pltpu
from jax.sharding import PartitionSpec as P

water_level = 4.0
eps = 1e-06
unroll = 8


def prepare_kernel(steps, count, owner_ref, library_ref, x_ref, inv_ref, out_ref, part, full, got, send_sems, recv_sems):
    me = lax.axis_index("tm")
    region = lax.axis_index("region")
    barrier = pltpu.get_barrier_semaphore()
    for d in range(1, count):
        peer = lax.rem(me + d, count)
        pl.semaphore_signal(barrier, inc=1, device_id=(peer, region), device_id_type=pl.DeviceIdType.MESH)

    panel = library_ref[...]
    taps = panel.shape[1]
    rows = panel.shape[0] // 16
    centred = panel - jnp.sum(panel, axis=1, keepdims=True) / taps
    normed = centred / jnp.sqrt(jnp.sum(centred * centred, axis=1, keepdims=True) + eps)
    mirror = lax.broadcasted_iota(jnp.int32, (taps, 256), 0) + lax.broadcasted_iota(jnp.int32, (taps, 256), 1)
    mirror = (mirror == 255).astype(jnp.float32).astype(jnp.bfloat16)
    turned = jnp.dot(normed.astype(jnp.bfloat16), mirror, preferred_element_type=jnp.float32)
    turned = turned.reshape(rows, 16, 256)
    if part.shape[0] > steps * rows:
        part[steps * rows :] = jnp.zeros((part.shape[0] - steps * rows, 16, 256), jnp.bfloat16)
    for s in range(steps):
        mine = jnp.where(owner_ref[s] == me, jnp.float32(1), jnp.float32(0))
        part[s * rows : (s + 1) * rows] = (turned * mine).astype(jnp.bfloat16)

    chans = x_ref.shape[0]
    blocks = x_ref.shape[1]
    group = 4
    chunks = chans // group
    offsets = lax.broadcasted_iota(jnp.int32, (384, 128), 0) - lax.broadcasted_iota(jnp.int32, (384, 128), 1)
    band = ((offsets >= 0) & (offsets < taps)).astype(jnp.float32).astype(jnp.bfloat16)

    def chunk(i, carry):
        x = x_ref[pl.ds(i * group, group)].reshape(group * blocks, 384).astype(jnp.float32)
        square = x * x
        high = square.astype(jnp.bfloat16)
        low = (square - high.astype(jnp.float32)).astype(jnp.bfloat16)
        energy = jnp.dot(high, band, preferred_element_type=jnp.float32)
        energy = energy + jnp.dot(low, band, preferred_element_type=jnp.float32)
        inv_ref[pl.ds(i * group, group)] = lax.rsqrt(energy + taps * water_level).reshape(group, blocks, 128)
        return carry

    phases = 2

    def scales(phase):
        lax.fori_loop(phase * chunks // phases, (phase + 1) * chunks // phases, chunk, 0)

    pl.semaphore_wait(barrier, count - 1)
    size = part.shape[0] // count
    own = pl.ds(me * size, size)

    def exchange(phase, source, target):
        copies = []
        for d in range(1, count):
            peer = lax.rem(me + d, count)
            copy = pltpu.make_async_remote_copy(
                src_ref=source(peer),
                dst_ref=target(d),
                send_sem=send_sems.at[phase, d - 1],
                recv_sem=recv_sems.at[phase, d - 1],
                device_id=(peer, region),
                device_id_type=pl.DeviceIdType.MESH,
            )
            copy.start()
            copies.append(copy)
        scales(phase)
        for copy in copies:
            copy.wait()

    exchange(0, lambda peer: part.at[pl.ds(peer * size, size)], lambda d: got.at[d - 1])
    total = part[own].astype(jnp.float32)
    for d in range(1, count):
        total = total + got[d - 1].astype(jnp.float32)
    full[own] = total.astype(jnp.bfloat16)
    exchange(1, lambda peer: full.at[own], lambda d: full.at[own])
    out_ref[...] = full[...].astype(jnp.float32)


def pair_kernel(code_ref, x_ref, inv_ref, taps_ref, out_ref, acc_ref, list_ref):
    templates = out_ref.shape[0]

    def compact(i, filled):
        code = code_ref[i]
        list_ref[filled] = code
        return filled + jnp.where(code >= 0, 1, 0)

    count = lax.fori_loop(0, code_ref.shape[0], compact, 0, unroll=8)
    for u in range(unroll):
        list_ref[count + u] = templates
    acc_ref[...] = jnp.zeros_like(acc_ref)
    lane = lax.broadcasted_iota(jnp.int32, (8, 128), 1)
    sub = lax.broadcasted_iota(jnp.int32, (8, 128), 0)

    def one_pair(code):
        template = code & 63
        col = (code >> 6) & 255
        row = code >> 14
        taps = taps_ref[pl.ds(row, 1), :]
        first = jnp.broadcast_to(taps[:, :128], (8, 128))
        second = jnp.broadcast_to(taps[:, 128:], (8, 128))
        first = pltpu.roll(first, 1, 1, stride=1, stride_axis=0)
        second = pltpu.roll(second, 1, 1, stride=1, stride_axis=0)
        zero = jnp.zeros((8, 128), jnp.float32)
        parts = [[], [], []]
        for a in range(16):
            one = pltpu.roll(first, 8 * a, 1) if a else first
            two = pltpu.roll(second, 8 * a, 1) if a else second
            below = lane <= sub + 8 * a
            parts[0].append(jnp.where(below, two, zero))
            parts[1].append(jnp.where(below, one, two))
            parts[2].append(jnp.where(below, zero, one))
        matrix = jnp.concatenate(parts[0] + parts[1] + parts[2], axis=0).astype(jnp.bfloat16)
        product = jnp.dot(x_ref[col], matrix, preferred_element_type=jnp.float32)
        return template, product * inv_ref[col]

    def group(i, carry):
        done = [one_pair(list_ref[i * unroll + u]) for u in range(unroll)]
        for template, value in done:
            acc_ref[template] += value
        return carry

    lax.fori_loop(0, (count + unroll - 1) // unroll, group, 0)
    out_ref[...] = acc_ref[:templates]


def finish_kernel(total_time, count, *refs):
    *parts, out_ref, sent, got, send_sems, recv_sems = refs
    me = lax.axis_index("tm")
    region = lax.axis_index("region")
    barrier = pltpu.get_barrier_semaphore()
    for d in range(1, count):
        peer = lax.rem(me + d, count)
        pl.semaphore_signal(barrier, inc=1, device_id=(peer, region), device_id_type=pl.DeviceIdType.MESH)
    held = out_ref.shape[0]
    stacked = parts[0][...]
    for other in parts[1:]:
        stacked = stacked + other[...]
    out_ref[...] = stacked
    power = jnp.sum(stacked * stacked, axis=1)
    power = jnp.broadcast_to(jnp.sum(power, axis=1, keepdims=True), (held, 128))
    sent[...] = power
    pl.semaphore_wait(barrier, count - 1)
    copies = []
    for d in range(1, count):
        peer = lax.rem(me + d, count)
        copy = pltpu.make_async_remote_copy(
            src_ref=sent,
            dst_ref=got.at[d - 1],
            send_sem=send_sems.at[d - 1],
            recv_sem=recv_sems.at[d - 1],
            device_id=(peer, region),
            device_id_type=pl.DeviceIdType.MESH,
        )
        copy.start()
        copies.append(copy)
    for copy in copies:
        copy.wait()
    power = power + jnp.sum(got[...], axis=0)
    factor = lax.rsqrt(power / total_time + eps)
    out_ref[...] = out_ref[...] * factor[:, None, :]


def pair_lists(station_order, channels, groups):
    steps, templates, used = channels.shape
    per_group = templates // groups
    length = steps * per_group * used
    grouped = channels.reshape(steps, groups, per_group, used).transpose(1, 0, 2, 3).reshape(groups, length)
    slot = jnp.arange(length, dtype=jnp.int32)
    step = slot // (per_group * used)
    inner = slot % (per_group * used)
    match = (grouped[:, :, None] == station_order[None, None, :]).astype(jnp.int32)
    local = jnp.sum(match, axis=2)
    col = jnp.sum(match * jnp.arange(station_order.shape[0], dtype=jnp.int32), axis=2)
    row = step * (templates * used) + jnp.arange(groups, dtype=jnp.int32)[:, None] * (per_group * used) + inner
    template = slot // used
    code = (row << 14) | (col << 6) | template
    return jnp.where(local > 0, code, -1)


def body(waveform, station_order, library, owner, channels):
    chan_local, time_local = waveform.shape
    num_blocks = time_local // 128
    steps, templates, used = channels.shape
    tap_count = library.shape[2]
    tm_size = lax.axis_size("tm")
    regions = lax.axis_size("region")
    per_group = templates // regions
    held = steps * per_group
    total_time = time_local * tm_size

    rim = lax.ppermute(waveform[:, :256], "tm", [(i, i - 1) for i in range(1, tm_size)])
    rim = jnp.where(jnp.arange(256)[None, :] < tap_count - 1, rim, jnp.zeros_like(rim))

    blocked = waveform.reshape(chan_local, num_blocks, 128)
    rim_blocks = rim.reshape(chan_local, 2, 128)
    extended = jnp.concatenate([blocked, rim_blocks], axis=1)
    windows = jnp.concatenate([extended[:, i : i + num_blocks] for i in range(3)], axis=2)

    vmem = pl.BlockSpec(memory_space=pltpu.VMEM)
    smem = pl.BlockSpec(memory_space=pltpu.SMEM)
    tap_rows = steps * templates * used
    tiles = -(-tap_rows // (16 * tm_size)) * tm_size
    tile = (tiles, 16, 256)
    inv_scale, taps = pl.pallas_call(
        functools.partial(prepare_kernel, steps, tm_size),
        out_shape=[
            jax.ShapeDtypeStruct((chan_local, num_blocks, 128), jnp.float32),
            jax.ShapeDtypeStruct(tile, jnp.float32),
        ],
        in_specs=[smem, vmem, vmem],
        out_specs=[vmem, vmem],
        scratch_shapes=[
            pltpu.VMEM(tile, jnp.bfloat16),
            pltpu.VMEM(tile, jnp.bfloat16),
            pltpu.VMEM((tm_size - 1, tiles // tm_size, 16, 256), jnp.bfloat16),
            pltpu.SemaphoreType.DMA((2, tm_size - 1)),
            pltpu.SemaphoreType.DMA((2, tm_size - 1)),
        ],
        compiler_params=pltpu.CompilerParams(
            collective_id=0, has_side_effects=True, vmem_limit_bytes=40 * 2**20
        ),
        name="prepare",
    )(owner, library.reshape(templates * used, tap_count), windows)
    taps = taps.reshape(tiles * 16, 256)

    codes = pair_lists(station_order, channels, regions)
    me = lax.axis_index("region")

    def partial_sums(group):
        return pl.pallas_call(
            pair_kernel,
            out_shape=jax.ShapeDtypeStruct((held, num_blocks, 128), jnp.float32),
            in_specs=[smem, vmem, vmem, vmem],
            out_specs=vmem,
            scratch_shapes=[
                pltpu.VMEM((held + 1, num_blocks, 128), jnp.float32),
                pltpu.SMEM((held * used + unroll,), jnp.int32),
            ],
            compiler_params=pltpu.CompilerParams(vmem_limit_bytes=40 * 2**20),
            cost_estimate=pl.CostEstimate(flops=held * used * 64 * 384 * 256, bytes_accessed=9 * 2**20, transcendentals=0),
            name="pairs",
        )(lax.dynamic_index_in_dim(codes, group, 0, False), windows, inv_scale, taps)

    arrived = []
    for shift in range(1, regions):
        part = partial_sums((me + shift) % regions)
        arrived.append(lax.ppermute(part, "region", [(i, (i + shift) % regions) for i in range(regions)]))
    arrived.append(partial_sums(me))
    result = pl.pallas_call(
        functools.partial(finish_kernel, total_time, tm_size),
        out_shape=jax.ShapeDtypeStruct((held, num_blocks, 128), jnp.float32),
        in_specs=[vmem] * len(arrived),
        out_specs=vmem,
        scratch_shapes=[
            pltpu.VMEM((held, 128), jnp.float32),
            pltpu.VMEM((tm_size - 1, held, 128), jnp.float32),
            pltpu.SemaphoreType.DMA((tm_size - 1,)),
            pltpu.SemaphoreType.DMA((tm_size - 1,)),
        ],
        compiler_params=pltpu.CompilerParams(
            collective_id=1, has_side_effects=True, vmem_limit_bytes=40 * 2**20
        ),
        name="finish",
    )(*arrived)
    return result.reshape(steps, per_group, time_local)


def solution(mesh):
    in_specs = (P("region", "tm"), P("region"), P("tm", None, None), P(), P())
    out_specs = P(None, "region", "tm")
    return jax.shard_map(body, mesh=mesh, in_specs=in_specs, out_specs=out_specs, check_vma=False)
```

```python
import functools
import jax
import jax.numpy as jnp
from jax import lax
from jax.experimental import pallas as pl
from jax.experimental.pallas import tpu as pltpu
from jax.sharding import PartitionSpec as P

water_level = 4.0
eps = 1e-06
unroll = 16


def prepare_kernel(steps, count, owner_ref, library_ref, x_ref, inv_ref, out_ref, part, full, got, send_sems, recv_sems):
    me = lax.axis_index("tm")
    region = lax.axis_index("region")
    barrier = pltpu.get_barrier_semaphore()
    for d in range(1, count):
        peer = lax.rem(me + d, count)
        pl.semaphore_signal(barrier, inc=1, device_id=(peer, region), device_id_type=pl.DeviceIdType.MESH)

    panel = library_ref[...]
    taps = panel.shape[1]
    rows = panel.shape[0] // 16
    centred = panel - jnp.sum(panel, axis=1, keepdims=True) / taps
    normed = centred / jnp.sqrt(jnp.sum(centred * centred, axis=1, keepdims=True) + eps)
    mirror = lax.broadcasted_iota(jnp.int32, (taps, 256), 0) + lax.broadcasted_iota(jnp.int32, (taps, 256), 1)
    mirror = (mirror == 255).astype(jnp.float32).astype(jnp.bfloat16)
    turned = jnp.dot(normed.astype(jnp.bfloat16), mirror, preferred_element_type=jnp.float32)
    turned = turned.reshape(rows, 16, 256)
    if part.shape[0] > steps * rows:
        part[steps * rows :] = jnp.zeros((part.shape[0] - steps * rows, 16, 256), jnp.bfloat16)
    for s in range(steps):
        mine = jnp.where(owner_ref[s] == me, jnp.float32(1), jnp.float32(0))
        part[s * rows : (s + 1) * rows] = (turned * mine).astype(jnp.bfloat16)

    chans = x_ref.shape[0]
    blocks = x_ref.shape[1]
    group = 4
    chunks = chans // group
    offsets = lax.broadcasted_iota(jnp.int32, (384, 128), 0) - lax.broadcasted_iota(jnp.int32, (384, 128), 1)
    band = ((offsets >= 0) & (offsets < taps)).astype(jnp.float32).astype(jnp.bfloat16)

    def chunk(i, carry):
        x = x_ref[pl.ds(i * group, group)].reshape(group * blocks, 384).astype(jnp.float32)
        square = x * x
        high = square.astype(jnp.bfloat16)
        low = (square - high.astype(jnp.float32)).astype(jnp.bfloat16)
        energy = jnp.dot(high, band, preferred_element_type=jnp.float32)
        energy = energy + jnp.dot(low, band, preferred_element_type=jnp.float32)
        inv_ref[pl.ds(i * group, group)] = lax.rsqrt(energy + taps * water_level).reshape(group, blocks, 128)
        return carry

    phases = 2

    def scales(phase):
        lax.fori_loop(phase * chunks // phases, (phase + 1) * chunks // phases, chunk, 0)

    pl.semaphore_wait(barrier, count - 1)
    size = part.shape[0] // count
    own = pl.ds(me * size, size)

    def exchange(phase, source, target):
        copies = []
        for d in range(1, count):
            peer = lax.rem(me + d, count)
            copy = pltpu.make_async_remote_copy(
                src_ref=source(peer),
                dst_ref=target(d),
                send_sem=send_sems.at[phase, d - 1],
                recv_sem=recv_sems.at[phase, d - 1],
                device_id=(peer, region),
                device_id_type=pl.DeviceIdType.MESH,
            )
            copy.start()
            copies.append(copy)
        scales(phase)
        for copy in copies:
            copy.wait()

    exchange(0, lambda peer: part.at[pl.ds(peer * size, size)], lambda d: got.at[d - 1])
    total = part[own].astype(jnp.float32)
    for d in range(1, count):
        total = total + got[d - 1].astype(jnp.float32)
    full[own] = total.astype(jnp.bfloat16)
    exchange(1, lambda peer: full.at[own], lambda d: full.at[own])
    out_ref[...] = full[...].astype(jnp.float32)


def pair_kernel(code_ref, x_ref, inv_ref, taps_ref, out_ref, acc_ref, list_ref):
    templates = out_ref.shape[0]

    def compact(i, filled):
        code = code_ref[i]
        list_ref[filled] = code
        return filled + jnp.where(code >= 0, 1, 0)

    count = lax.fori_loop(0, code_ref.shape[0], compact, 0, unroll=8)
    for u in range(unroll):
        list_ref[count + u] = templates
    acc_ref[...] = jnp.zeros_like(acc_ref)
    lane = lax.broadcasted_iota(jnp.int32, (8, 128), 1)
    sub = lax.broadcasted_iota(jnp.int32, (8, 128), 0)

    def one_pair(code):
        template = code & 63
        col = (code >> 6) & 255
        row = code >> 14
        taps = taps_ref[pl.ds(row, 1), :]
        first = jnp.broadcast_to(taps[:, :128], (8, 128))
        second = jnp.broadcast_to(taps[:, 128:], (8, 128))
        first = pltpu.roll(first, 1, 1, stride=1, stride_axis=0)
        second = pltpu.roll(second, 1, 1, stride=1, stride_axis=0)
        zero = jnp.zeros((8, 128), jnp.float32)
        parts = [[], [], []]
        for a in range(16):
            one = pltpu.roll(first, 8 * a, 1) if a else first
            two = pltpu.roll(second, 8 * a, 1) if a else second
            below = lane <= sub + 8 * a
            parts[0].append(jnp.where(below, two, zero))
            parts[1].append(jnp.where(below, one, two))
            parts[2].append(jnp.where(below, zero, one))
        matrix = jnp.concatenate(parts[0] + parts[1] + parts[2], axis=0).astype(jnp.bfloat16)
        product = jnp.dot(x_ref[col], matrix, preferred_element_type=jnp.float32)
        return template, product * inv_ref[col]

    def group(i, carry):
        done = [one_pair(list_ref[i * unroll + u]) for u in range(unroll)]
        for template, value in done:
            acc_ref[template] += value
        return carry

    lax.fori_loop(0, (count + unroll - 1) // unroll, group, 0)
    out_ref[...] = acc_ref[:templates]


def finish_kernel(total_time, count, *refs):
    *parts, out_ref, sent, got, send_sems, recv_sems = refs
    me = lax.axis_index("tm")
    region = lax.axis_index("region")
    barrier = pltpu.get_barrier_semaphore()
    for d in range(1, count):
        peer = lax.rem(me + d, count)
        pl.semaphore_signal(barrier, inc=1, device_id=(peer, region), device_id_type=pl.DeviceIdType.MESH)
    held = out_ref.shape[0]
    stacked = parts[0][...]
    for other in parts[1:]:
        stacked = stacked + other[...]
    out_ref[...] = stacked
    power = jnp.sum(stacked * stacked, axis=1)
    power = jnp.broadcast_to(jnp.sum(power, axis=1, keepdims=True), (held, 128))
    sent[...] = power
    pl.semaphore_wait(barrier, count - 1)
    copies = []
    for d in range(1, count):
        peer = lax.rem(me + d, count)
        copy = pltpu.make_async_remote_copy(
            src_ref=sent,
            dst_ref=got.at[d - 1],
            send_sem=send_sems.at[d - 1],
            recv_sem=recv_sems.at[d - 1],
            device_id=(peer, region),
            device_id_type=pl.DeviceIdType.MESH,
        )
        copy.start()
        copies.append(copy)
    for copy in copies:
        copy.wait()
    power = power + jnp.sum(got[...], axis=0)
    factor = lax.rsqrt(power / total_time + eps)
    out_ref[...] = out_ref[...] * factor[:, None, :]


def pair_lists(station_order, channels, groups):
    steps, templates, used = channels.shape
    per_group = templates // groups
    length = steps * per_group * used
    grouped = channels.reshape(steps, groups, per_group, used).transpose(1, 0, 2, 3).reshape(groups, length)
    slot = jnp.arange(length, dtype=jnp.int32)
    step = slot // (per_group * used)
    inner = slot % (per_group * used)
    match = (grouped[:, :, None] == station_order[None, None, :]).astype(jnp.int32)
    local = jnp.sum(match, axis=2)
    col = jnp.sum(match * jnp.arange(station_order.shape[0], dtype=jnp.int32), axis=2)
    row = step * (templates * used) + jnp.arange(groups, dtype=jnp.int32)[:, None] * (per_group * used) + inner
    template = slot // used
    code = (row << 14) | (col << 6) | template
    return jnp.where(local > 0, code, -1)


def body(waveform, station_order, library, owner, channels):
    chan_local, time_local = waveform.shape
    num_blocks = time_local // 128
    steps, templates, used = channels.shape
    tap_count = library.shape[2]
    tm_size = lax.axis_size("tm")
    regions = lax.axis_size("region")
    per_group = templates // regions
    held = steps * per_group
    total_time = time_local * tm_size

    rim = lax.ppermute(waveform[:, :256], "tm", [(i, i - 1) for i in range(1, tm_size)])
    rim = jnp.where(jnp.arange(256)[None, :] < tap_count - 1, rim, jnp.zeros_like(rim))

    blocked = waveform.reshape(chan_local, num_blocks, 128)
    rim_blocks = rim.reshape(chan_local, 2, 128)
    extended = jnp.concatenate([blocked, rim_blocks], axis=1)
    windows = jnp.concatenate([extended[:, i : i + num_blocks] for i in range(3)], axis=2)

    vmem = pl.BlockSpec(memory_space=pltpu.VMEM)
    smem = pl.BlockSpec(memory_space=pltpu.SMEM)
    tap_rows = steps * templates * used
    tiles = -(-tap_rows // (16 * tm_size)) * tm_size
    tile = (tiles, 16, 256)
    inv_scale, taps = pl.pallas_call(
        functools.partial(prepare_kernel, steps, tm_size),
        out_shape=[
            jax.ShapeDtypeStruct((chan_local, num_blocks, 128), jnp.float32),
            jax.ShapeDtypeStruct(tile, jnp.float32),
        ],
        in_specs=[smem, vmem, vmem],
        out_specs=[vmem, vmem],
        scratch_shapes=[
            pltpu.VMEM(tile, jnp.bfloat16),
            pltpu.VMEM(tile, jnp.bfloat16),
            pltpu.VMEM((tm_size - 1, tiles // tm_size, 16, 256), jnp.bfloat16),
            pltpu.SemaphoreType.DMA((2, tm_size - 1)),
            pltpu.SemaphoreType.DMA((2, tm_size - 1)),
        ],
        compiler_params=pltpu.CompilerParams(
            collective_id=0, has_side_effects=True, vmem_limit_bytes=40 * 2**20
        ),
        name="prepare",
    )(owner, library.reshape(templates * used, tap_count), windows)
    taps = taps.reshape(tiles * 16, 256)

    codes = pair_lists(station_order, channels, regions)
    me = lax.axis_index("region")

    def partial_sums(group):
        return pl.pallas_call(
            pair_kernel,
            out_shape=jax.ShapeDtypeStruct((held, num_blocks, 128), jnp.float32),
            in_specs=[smem, vmem, vmem, vmem],
            out_specs=vmem,
            scratch_shapes=[
                pltpu.VMEM((held + 1, num_blocks, 128), jnp.float32),
                pltpu.SMEM((held * used + unroll,), jnp.int32),
            ],
            compiler_params=pltpu.CompilerParams(vmem_limit_bytes=40 * 2**20),
            cost_estimate=pl.CostEstimate(flops=held * used * 64 * 384 * 256, bytes_accessed=9 * 2**20, transcendentals=0),
            name="pairs",
        )(lax.dynamic_index_in_dim(codes, group, 0, False), windows, inv_scale, taps)

    arrived = []
    for shift in range(1, regions):
        part = partial_sums((me + shift) % regions)
        arrived.append(lax.ppermute(part, "region", [(i, (i + shift) % regions) for i in range(regions)]))
    arrived.append(partial_sums(me))
    result = pl.pallas_call(
        functools.partial(finish_kernel, total_time, tm_size),
        out_shape=jax.ShapeDtypeStruct((held, num_blocks, 128), jnp.float32),
        in_specs=[vmem] * len(arrived),
        out_specs=vmem,
        scratch_shapes=[
            pltpu.VMEM((held, 128), jnp.float32),
            pltpu.VMEM((tm_size - 1, held, 128), jnp.float32),
            pltpu.SemaphoreType.DMA((tm_size - 1,)),
            pltpu.SemaphoreType.DMA((tm_size - 1,)),
        ],
        compiler_params=pltpu.CompilerParams(
            collective_id=1, has_side_effects=True, vmem_limit_bytes=40 * 2**20
        ),
        name="finish",
    )(*arrived)
    return result.reshape(steps, per_group, time_local)


def solution(mesh):
    in_specs = (P("region", "tm"), P("region"), P("tm", None, None), P(), P())
    out_specs = P(None, "region", "tm")
    return jax.shard_map(body, mesh=mesh, in_specs=in_specs, out_specs=out_specs, check_vma=False)
```
